32 devices in a mesh: ctx: 8 (over z, core), exp: 4 (over y, x).
Axes of the slice: x: 2, y: 2, z: 4, core: 2. Of those that a mesh axis runs over, the one named last changes fastest.
Arguments:
- queries: bfloat16 [4, 1024, 2048], P('exp', 'ctx'), may hold values from -18 to 18
- keys: bfloat16 [4, 1024, 2048], P('exp', 'ctx'), may hold values from -18 to 18
- values: bfloat16 [4, 1024, 2048], P('exp', 'ctx'), may hold values from -7 to 7
- segment_ids: int32 [4, 1024], P('exp', 'ctx'), may hold values from 0 to 2, never falling along the last dimension, each value on 1 to 512 neighbouring positions
- hidden_in: bfloat16 [4, 1024, 2048], P('exp', 'ctx'), may hold values from -6 to 6
- out_weight: bfloat16 [2048, 2048], replicated, may hold values from -0.125 to 0.125
- norm_gain: float32 [2048], replicated, may hold values from 0.25 to 1.75
- expert_ids: int32 [4, 1024, 6], P('exp', 'ctx'), may hold values from 0 to 15, all different within a row; in each aligned block of 128 rows (0 to 127, 128 to 255, ..., all dimensions but the last counted through in order) at most 64 rows name the same one
- gate_codes: int32 [4, 1024, 6], P('exp', 'ctx'), may hold values from 1 to 64
- w_in: bfloat16 [32, 2048, 1408], P(('ctx', 'exp')), may hold values from -0.125 to 0.125
- w_down: bfloat16 [32, 704, 2048], P(('ctx', 'exp')), may hold values from -0.15625 to 0.15625
Outputs:
- layer_out: bfloat16 [4, 1024, 2048], P('exp', 'ctx')
The draws below stay inside these ranges and needn't reach their ends.
Inputs may be any that keep to these rules, and one draw needn't show every extreme that they name: `segment_ids`: segment numbers never fall along a stream; every segment has at most 512 positions and some segment of each stream has exactly 512. `expert_ids`: each token names 6 different experts; among the tokens of one device no expert is named more than 64 times, and some device reaches 64.
All inputs are finite; a program needn't handle non-finite values.
Results may differ from the reference program's by a relative error of at most 0.0095.
Values may be sent and summed in bfloat16 or wider, within the bound.
A program may use at most 128 MiB of HBM per device.

```python
import math
import jax
import jax.numpy as jnp
import numpy as np
from jax import lax

D = 2048
HEADS = 16
HEAD_DIM = 128
FF = 1408
TOPK = 6
TOK_DEV = 128
SEG_COUNT = 3
STREAMS = 4
SEQ = 1024
SEG_MOST = 512
EXPERTS = 16
HALF = 704
ROUTE_MOST = 64
DEVICES = 32


def drawn_pair(key):
    shape = (STREAMS, SEQ, D)
    base_query = jnp.clip(jax.random.normal(jax.random.fold_in(key, 11), shape, jnp.float32), -4.0, 4.0)
    base_key = jnp.clip(jax.random.normal(jax.random.fold_in(key, 12), shape, jnp.float32), -4.0, 4.0)
    return (base_query, base_key)


def draw_queries(key, part):
    return drawn_pair(key)[0].astype(jnp.bfloat16)


def draw_keys(key, part):
    return drawn_pair(key)[1].astype(jnp.bfloat16)


def draw_values(key, part):
    shape = (STREAMS, SEQ, D)
    base = jnp.clip(jax.random.normal(jax.random.fold_in(key, 21), shape, jnp.float32), -4.0, 4.0)
    offset = jnp.clip(jax.random.normal(jax.random.fold_in(key, 22), (STREAMS, SEQ // TOK_DEV, 1, D), jnp.float32), -3.0, 3.0)
    spread_offset = jnp.broadcast_to(offset, (STREAMS, SEQ // TOK_DEV, TOK_DEV, D)).reshape(shape)
    return (base + spread_offset).astype(jnp.bfloat16)


def with_ends(drawn, own_key, low, high):
    spot = [jax.random.randint(jax.random.fold_in(own_key, axis), (), 0, length) for axis, length in enumerate(drawn.shape)]
    longest = drawn.shape.index(max(drawn.shape))
    next_to = spot[:longest] + [(spot[longest] + 1) % drawn.shape[longest]] + spot[longest + 1:]
    return drawn.at[tuple(spot)].set(low).at[tuple(next_to)].set(high)


def levels(rng, dims, shards, smallest, high):
    def one(dim, shards_of):
        heights = jax.random.uniform(jax.random.fold_in(jax.random.fold_in(rng, 6), dim), (shards_of,), jnp.float32, smallest / len(shards), high / len(shards))
        return jnp.repeat(jnp.exp(heights), dims[dim] // shards_of).reshape((-1,) + (1,) * (len(dims) - dim - 1))

    factor_of = one(*shards[0])
    for cut in shards[1:]:
        factor_of = factor_of * one(*cut)
    return factor_of


def split_up(number_of, total, most, lean):
    loads = [(1 << 20) // math.isqrt(standing ** lean) + 1 for standing in range(2, number_of + 1)]
    surplus, given = total - most - (number_of - 1), [1] * (number_of - 1)
    while surplus > 0:
        candidates = [i for i in range(number_of - 1) if given[i] < most]
        mass, left = sum([loads[i] for i in candidates]), surplus
        for i in candidates:
            extra = min(most - given[i], max(1, left * loads[i] // mass), surplus)
            given[i] = given[i] + extra
            surplus = surplus - extra
    return np.array([most] + given)


def ragged_sizes(key, amount, total, limit, slope):
    if amount == 2:
        one = jax.random.randint(key, (), max(1, total - limit), min(limit, total - 1) + 1)
        return jnp.stack([one, total - one])
    lengths = jnp.asarray(split_up(amount, total, limit, slope), jnp.int32)
    couples = (amount - 1) // 2
    giver, sink = lengths[1:1 + 2 * couples:2], lengths[2:2 + 2 * couples:2]
    margin = jnp.minimum(giver - 1, limit - sink)
    moved = jax.random.randint(jax.random.fold_in(key, 1), (couples,), 0, 1 << 20) % (margin + 1)
    lengths = lengths.at[1:1 + 2 * couples:2].set(giver - moved).at[2:2 + 2 * couples:2].set(sink + moved)
    return lengths[jax.random.permutation(jax.random.fold_in(key, 2), amount)]


def routed_block(rng, own, number, rows, number_of, top, bound, slope):
    sequence = jax.random.permutation(rng, number_of)
    crowded, ordinary = shares(number_of, rows * top, bound, slope, True), shares(number_of, rows * top, bound, slope, False)
    places = jnp.arange(number_of)

    def named(tallies, offset_by):
        used = int((tallies > 0).sum())
        fixed = max(1, used // 4)
        moved = fixed + (places - fixed + offset_by * (used - fixed)) % max(1, number_of - fixed)
        return jnp.zeros((number_of,), jnp.int32).at[sequence[jnp.where(places < fixed, places, moved)]].set(jnp.asarray(tallies, jnp.int32))

    tallies = jnp.where(number % 4 == 0, named(crowded, number // 4), named(ordinary, number - number // 4 - 1))
    mixed = jax.random.permutation(jax.random.fold_in(own, 3), number_of)
    giver, taker = mixed[0:number_of // 2 * 2:2], mixed[1:number_of // 2 * 2:2]
    margin = jnp.minimum(tallies[giver] - 1, bound - tallies[taker]) // 2
    margin = jnp.where((giver == sequence[0]) | (taker == sequence[0]) | (tallies[taker] == 0), 0, jnp.maximum(margin, 0))
    moved = jax.random.randint(jax.random.fold_in(own, 4), (number_of // 2,), 0, 1 << 20) % (margin + 1)
    tallies = tallies.at[giver].add(-moved).at[taker].add(moved)
    labels = jnp.searchsorted(jnp.cumsum(tallies), jnp.arange(rows * top), side="right").astype(jnp.int32)
    table = labels.reshape(top, rows).T
    table = table[jax.random.permutation(jax.random.fold_in(own, 1), rows)]
    offset_by = jax.random.randint(jax.random.fold_in(own, 2), (rows, 1), 0, top)
    return jnp.take_along_axis(table, (jnp.arange(top)[None, :] + offset_by) % top, axis=1)


def shares(number_of, total, most, skew, full):
    loads = [(1 << 20) // math.isqrt(grade ** skew) + 1 for grade in range(1, number_of + 1)]
    largest = most if full else min(most, max(-(-total // number_of), total * loads[0] // sum(loads)))
    least = 1 if total - largest >= number_of - 1 else 0
    counts, spare = [largest] + [least] * (number_of - 1), total - largest - least * (number_of - 1)
    while spare > 0:
        movable = [i for i in range(1, number_of) if counts[i] < largest] or [i for i in range(1, number_of) if counts[i] < most]
        whole, remaining = sum([loads[i] for i in movable]), spare
        for i in movable:
            extra = min(most - counts[i], max(1, remaining * loads[i] // whole), spare)
            counts[i] = counts[i] + extra
            spare = spare - extra
    return np.array(counts)


def normal_values(rng, shape, scale, most, shards=(), kind=jnp.bfloat16):
    drawn = jax.random.normal(rng, shape, jnp.float32) * scale
    if len(shards) > 0:
        drawn = levels(rng, shape, shards, -0.22, 0.18) * drawn
    return jnp.clip(drawn, min=-most, max=most).astype(kind)


def setup_inputs(seed: int = 0) -> dict:
    seeds = jax.random.split(jax.random.key(seed), 12)
    queries = draw_queries(jax.random.fold_in(seeds[11], 71), 0)
    keys = draw_keys(jax.random.fold_in(seeds[11], 71), 0)
    values = draw_values(jax.random.fold_in(seeds[11], 71), 0)
    segment_ids = jax.vmap(lambda own: jnp.searchsorted(jnp.cumsum(ragged_sizes(own, SEG_COUNT, SEQ, SEG_MOST, 1)), jnp.arange(SEQ), side="right"))(jax.random.split(seeds[3], STREAMS)).reshape((STREAMS, SEQ)).astype(jnp.int32)
    hidden_in = normal_values(seeds[4], (STREAMS, SEQ, D), 1.0, 6.0, ((0, 4), (1, 8)))
    out_weight = normal_values(seeds[5], (D, D), D ** -0.5, 0.125)
    norm_gain = jnp.clip(1.0 + 0.15 * jax.random.normal(seeds[6], (D,), jnp.float32), 0.25, 1.75)
    expert_ids_keys = jax.random.split(jax.random.fold_in(seeds[7], 1), STREAMS * SEQ // TOK_DEV)
    expert_ids_turns = jax.random.permutation(jax.random.fold_in(seeds[7], 3), STREAMS * SEQ // TOK_DEV)
    expert_ids = jax.vmap(lambda own, number: routed_block(jax.random.fold_in(seeds[7], 2), own, number, TOK_DEV, EXPERTS, TOPK, ROUTE_MOST, 2))(expert_ids_keys, expert_ids_turns).reshape((STREAMS, SEQ, TOPK))
    gate_codes = with_ends(jax.random.randint(seeds[8], (STREAMS, SEQ, TOPK), 1, 65), jax.random.fold_in(seeds[8], 1), 1, 64).astype(jnp.int32)
    w_in = normal_values(seeds[9], (DEVICES, D, FF), D ** -0.5, 0.125, ((0, 32),))
    w_down = normal_values(seeds[10], (DEVICES, HALF, D), FF ** -0.5, 0.15625, ((0, 32),))
    return dict(queries=queries, keys=keys, values=values, segment_ids=segment_ids, hidden_in=hidden_in, out_weight=out_weight, norm_gain=norm_gain, expert_ids=expert_ids, gate_codes=gate_codes, w_in=w_in, w_down=w_down)


def attend_stream(query_rows, key_rows, value_rows, seg_row):
    scale = HEAD_DIM ** (-0.5)
    query_heads = query_rows.astype(jnp.float32).reshape(SEQ, HEADS, HEAD_DIM)
    key_heads = key_rows.astype(jnp.float32).reshape(SEQ, HEADS, HEAD_DIM)
    value_heads = value_rows.astype(jnp.float32).reshape(SEQ, HEADS, HEAD_DIM)
    position = jnp.arange(SEQ, dtype=jnp.int32)
    block_rows = min(512, SEQ)
    pieces = []
    for block_index in range(SEQ // block_rows):
        first = block_index * block_rows
        query_block = query_heads[first:first + block_rows]
        scores = jnp.einsum('qhd,khd->hqk', query_block, key_heads) * scale
        allowed = (position[None, :] <= position[first:first + block_rows, None]) & (seg_row[None, :] == seg_row[first:first + block_rows, None])
        scores = jnp.where(allowed[None], scores, -jnp.inf)
        row_top = lax.optimization_barrier(jnp.max(scores, axis=-1, keepdims=True))
        probs = jnp.where(allowed[None], jnp.exp(scores - row_top), 0.0)
        total = lax.optimization_barrier(jnp.sum(probs, axis=-1))
        probs_low = lax.optimization_barrier(probs.astype(jnp.bfloat16)).astype(jnp.float32)
        weighted = jnp.einsum('hqk,khd->qhd', probs_low, value_heads)
        pieces.append(weighted / total.T[:, :, None])
    return jnp.concatenate(pieces, axis=0).reshape(SEQ, D).astype(jnp.bfloat16)

def reference(queries, keys, values, segment_ids, hidden_in, out_weight, norm_gain, expert_ids, gate_codes, w_in, w_down):
    attended = jnp.stack([attend_stream(queries[stream], keys[stream], values[stream], segment_ids[stream]) for stream in range(STREAMS)])
    projected = jnp.dot(attended.reshape(STREAMS * SEQ, D), out_weight, preferred_element_type=jnp.float32)
    mixed = (hidden_in.reshape(STREAMS * SEQ, D).astype(jnp.float32) + projected).astype(jnp.bfloat16)
    mixed_wide = mixed.astype(jnp.float32)
    normed = (mixed_wide * lax.rsqrt(lax.optimization_barrier(jnp.mean(mixed_wide * mixed_wide, axis=-1, keepdims=True)) + 1e-06) * norm_gain).astype(jnp.bfloat16)
    token_count = STREAMS * SEQ
    blocks = token_count // TOK_DEV
    normed_pad = jnp.concatenate([normed, jnp.zeros((1, D), jnp.bfloat16)], axis=0)
    flat_ids = expert_ids.reshape(token_count * TOPK).astype(jnp.int32)
    onehot = (flat_ids.reshape(blocks, TOK_DEV * TOPK, 1) == jnp.arange(EXPERTS, dtype=jnp.int32)[None, None, :]).astype(jnp.int32)
    ranks = lax.optimization_barrier(jnp.sum(jnp.cumsum(onehot, axis=1) * onehot, axis=-1)) - 1
    assign = jnp.arange(token_count * TOPK, dtype=jnp.int32)
    slot_flat = (ranks.reshape(-1) + assign // (TOK_DEV * TOPK) * ROUTE_MOST).astype(jnp.int32)
    token_index = (assign // TOPK).astype(jnp.int32)
    table = jnp.full((EXPERTS, blocks * ROUTE_MOST), token_count, jnp.int32).at[flat_ids, slot_flat].set(token_index)
    codes = gate_codes.astype(jnp.float32)
    route_weight = (codes / lax.optimization_barrier(jnp.sum(codes, axis=-1, keepdims=True))).reshape(-1)
    weight_table = jnp.zeros((EXPERTS, blocks * ROUTE_MOST), jnp.float32).at[flat_ids, slot_flat].set(route_weight)
    w_in_pairs = w_in.reshape(EXPERTS, 2, D, FF)
    w_down_pairs = w_down.reshape(EXPERTS, 2, HALF, D)

    def expert_step(running, inputs):
        row_index, row_weight, gate_up, down_rows = inputs
        gathered = normed_pad[row_index]
        expert_sum = jnp.zeros((row_index.shape[0], D), jnp.float32)
        for half_index in range(2):
            inner = jnp.dot(gathered, gate_up[half_index], preferred_element_type=jnp.float32)
            act = (jax.nn.silu(inner[:, :HALF]) * inner[:, HALF:]).astype(jnp.bfloat16)
            part = jnp.dot(act, down_rows[half_index], preferred_element_type=jnp.float32).astype(jnp.bfloat16)
            expert_sum = expert_sum + lax.optimization_barrier(part).astype(jnp.float32)
        running = running.at[row_index].add(row_weight[:, None] * expert_sum)
        return (running, None)
    start_total = jnp.zeros((token_count + 1, D), jnp.float32)
    routed, leftover = lax.scan(expert_step, start_total, (table, weight_table, w_in_pairs, w_down_pairs))
    layer_out = (mixed_wide + routed[:token_count]).astype(jnp.bfloat16)
    return layer_out.reshape(STREAMS, SEQ, D)
```

```python
import functools

import jax
import jax.numpy as jnp
from jax import lax
from jax.experimental import pallas as pl
from jax.experimental.pallas import tpu as pltpu
from jax.sharding import PartitionSpec as P

D = 2048
HEADS = 16
HEAD_DIM = 128
TOPK = 6
CHUNKS = 2
GROUP = 4

NEG_FILL = -1e30
BOTH = ("ctx", "exp")


def hop(block):
    devices = range(lax.axis_size("ctx"))
    return lax.ppermute(block, "ctx", [(i, i + 2) for i in devices if i + 2 in devices])


def swap(block):
    devices = range(lax.axis_size("ctx"))
    return lax.ppermute(block, "ctx", [(i, i ^ 1) for i in devices])


def attend_kernel(count, mask_ref, q_ref, *refs):
    k_refs, v_refs, out_ref = refs[:count], refs[count : 2 * count], refs[2 * count]
    allowed = mask_ref[...] > 0.0
    for head in range(GROUP):
        cols = slice(head * HEAD_DIM, (head + 1) * HEAD_DIM)
        query = q_ref[:, cols]
        scores = jnp.concatenate(
            [
                lax.dot_general(
                    query, k[:, cols], (((1,), (1,)), ((), ())), preferred_element_type=jnp.float32
                )
                for k in k_refs
            ],
            axis=1,
        ) * HEAD_DIM ** (-0.5)
        scores = jnp.where(allowed, scores, NEG_FILL)
        top = jnp.max(scores, axis=1, keepdims=True)
        probs = jnp.where(allowed, jnp.exp(scores - top), 0.0)
        total = jnp.sum(probs, axis=1, keepdims=True)
        low = probs.astype(jnp.bfloat16)
        rows = k_refs[0].shape[0]
        acc = sum(
            jnp.dot(
                low[:, i * rows : (i + 1) * rows], v[:, cols], preferred_element_type=jnp.float32
            )
            for i, v in enumerate(v_refs)
        )
        out_ref[:, cols] = (acc / total).astype(jnp.bfloat16)


def attend(mask, query, key_blocks, value_blocks):
    rows, width = query.shape
    count = len(key_blocks)
    wide = GROUP * HEAD_DIM
    block = pl.BlockSpec((rows, wide), lambda i: (0, i))
    return pl.pallas_call(
        functools.partial(attend_kernel, count),
        grid=(width // wide,),
        in_specs=[pl.BlockSpec(mask.shape, lambda i: (0, 0))] + [block] * (1 + 2 * count),
        out_specs=block,
        out_shape=jax.ShapeDtypeStruct((rows, width), jnp.bfloat16),
        compiler_params=pltpu.CompilerParams(vmem_limit_bytes=32 * 1024 * 1024),
        cost_estimate=pl.CostEstimate(
            flops=4 * rows * rows * count * width,
            bytes_accessed=4 * rows * width * (count + 1),
            transcendentals=rows * rows * count * HEADS,
        ),
    )(mask, query, *key_blocks, *value_blocks)


def gather_blocks(block):
    steps = lax.axis_size("ctx") // 4
    first = lax.axis_index("ctx") % 2 == 0
    chain = [block]
    for _ in range(steps):
        chain.append(hop(chain[-1]))
    others = [swap(chain[k]) for k in range(1, steps)]
    return chain + others + [swap(jnp.where(first, chain[0], chain[-1]))]


def expert_half(tokens, gate_up, down_rows):
    half = down_rows.shape[0]
    inner = jnp.dot(tokens, gate_up, preferred_element_type=jnp.float32)
    act = (jax.nn.silu(inner[:, :half]) * inner[:, half:]).astype(jnp.bfloat16)
    return jnp.dot(act, down_rows, preferred_element_type=jnp.float32)


def earlier(rows):
    order = jnp.arange(rows)
    return (order[:, None] < order[None, :]).astype(jnp.bfloat16)


def routed_by_gather(normed, meta, w_in, w_down):
    rows = normed.shape[0]
    owners = meta.shape[0]
    owner = lax.axis_index("ctx") * lax.axis_size("exp") + lax.axis_index("exp")
    ids, codes = meta[:, :TOPK] // 128, (meta[:, :TOPK] % 128).astype(jnp.float32)
    hit = jnp.where(ids == owner // 2, codes, 0.0)
    weight = jnp.sum(hit, axis=1) / jnp.sum(codes, axis=1)
    part_rows = rows // CHUNKS
    pieces = []
    for c in range(CHUNKS):
        span = slice(c * part_rows, (c + 1) * part_rows)
        tokens = lax.all_gather(normed[span], BOTH, axis=0, tiled=True)
        part = expert_half(tokens, w_in, w_down)
        share = weight[:, span].reshape(owners * part_rows, 1)
        part = jnp.where(share > 0.0, part * share, 0.0).astype(jnp.bfloat16)
        pieces.append(lax.psum_scatter(part, BOTH, scatter_dimension=0, tiled=True))
    return jnp.concatenate(pieces, axis=0).astype(jnp.float32)


def routed_by_exchange(normed, ids, codes, capacity, w_in, w_down):
    rows = normed.shape[0]
    owners = lax.axis_size("ctx") * lax.axis_size("exp")
    experts = owners // 2
    codes = codes.astype(jnp.float32)
    route = codes / jnp.sum(codes, axis=1, keepdims=True)
    named = ids[:, :, None] == jnp.arange(experts, dtype=jnp.int32)
    member = jnp.any(named, axis=1)
    weight = jnp.sum(jnp.where(named, route[:, :, None], 0.0), axis=1)
    rank = jnp.einsum(
        "st,se->te", earlier(rows), member.astype(jnp.bfloat16), preferred_element_type=jnp.float32
    ).astype(jnp.int32)
    slot = jnp.where(member, rank, -1).T[:, None, :]
    chosen = slot == jnp.arange(capacity, dtype=jnp.int32)[None, :, None]
    sent = jnp.einsum(
        "ect,td->ecd", chosen.astype(jnp.bfloat16), normed, preferred_element_type=jnp.float32
    ).astype(jnp.bfloat16)
    sent = jnp.broadcast_to(sent[:, None], (experts, 2, capacity, D)).reshape(owners, capacity, D)
    got = lax.all_to_all(sent, BOTH, split_axis=0, concat_axis=0, tiled=True)
    part = expert_half(got.reshape(owners * capacity, D), w_in, w_down).astype(jnp.bfloat16)
    back = lax.all_to_all(
        part.reshape(owners, capacity, D), BOTH, split_axis=0, concat_axis=0, tiled=True
    ).reshape(experts, 2, capacity, D)
    expert_out = back[:, 0].astype(jnp.float32) + back[:, 1].astype(jnp.float32)
    spread = jnp.where(chosen, weight.T[:, None, :], 0.0)
    return jnp.einsum("ect,ecd->td", spread, expert_out, precision=lax.Precision.HIGHEST)


def local(
    queries,
    keys,
    values,
    segment_ids,
    hidden_in,
    out_weight,
    norm_gain,
    expert_ids,
    gate_codes,
    w_in,
    w_down,
):
    rows = queries.shape[1]
    ctx_size = lax.axis_size("ctx")
    exp_size = lax.axis_size("exp")
    owners = ctx_size * exp_size
    capacity = rows * TOPK * 8 // (3 * owners)
    me = lax.axis_index("ctx")
    packed = (expert_ids[0] * 128 + gate_codes[0]).T
    meta = lax.all_gather(
        jnp.concatenate([packed, segment_ids, segment_ids], axis=0), BOTH, axis=0, tiled=False
    )
    segs = lax.dynamic_index_in_dim(
        meta[:, TOPK].reshape(ctx_size, exp_size, rows), lax.axis_index("exp"), 1, keepdims=False
    )
    steps = ctx_size // 4
    other = me + 1 - 2 * (me % 2)
    whose = jnp.stack(
        [me - 2 * k for k in range(steps + 1)]
        + [other - 2 * k for k in range(1, steps)]
        + [jnp.where(me % 2 == 0, other - 2 * steps, other)]
    )
    key_pos = (whose[:, None] * rows + jnp.arange(rows, dtype=jnp.int32)).reshape(-1)
    key_seg = segs[jnp.maximum(whose, 0)].reshape(-1)
    query_pos = me * rows + jnp.arange(rows, dtype=jnp.int32)
    mask = (
        (key_pos[None, :] <= query_pos[:, None])
        & (key_pos[None, :] >= 0)
        & (key_seg[None, :] == segment_ids[0][:, None])
    ).astype(jnp.float32)
    attended = attend(mask, queries[0], gather_blocks(keys[0]), gather_blocks(values[0]))
    projected = jnp.dot(attended, out_weight, preferred_element_type=jnp.float32)
    mixed_wide = (
        (hidden_in[0].astype(jnp.float32) + projected).astype(jnp.bfloat16).astype(jnp.float32)
    )
    normed = (
        mixed_wide
        * lax.rsqrt(jnp.mean(mixed_wide * mixed_wide, axis=-1, keepdims=True) + 1e-06)
        * norm_gain
    ).astype(jnp.bfloat16)
    if 2 * capacity >= rows:
        routed = routed_by_gather(normed, meta, w_in[0], w_down[0])
    else:
        routed = routed_by_exchange(
            normed, expert_ids[0], gate_codes[0], capacity, w_in[0], w_down[0]
        )
    return (mixed_wide + routed).astype(jnp.bfloat16)[None]


def solution(mesh):
    placed = (
        P("exp", "ctx", None),
        P("exp", "ctx", None),
        P("exp", "ctx", None),
        P("exp", "ctx"),
        P("exp", "ctx", None),
        P(),
        P(),
        P("exp", "ctx", None),
        P("exp", "ctx", None),
        P(("ctx", "exp"), None, None),
        P(("ctx", "exp"), None, None),
    )
    return jax.shard_map(
        local, mesh=mesh, in_specs=placed, out_specs=P("exp", "ctx", None), check_vma=False
    )
```

```python
import functools

import jax
import jax.numpy as jnp
from jax import lax
from jax.experimental import pallas as pl
from jax.experimental.pallas import tpu as pltpu
from jax.sharding import PartitionSpec as P

D = 2048
HEADS = 16
HEAD_DIM = 128
TOPK = 6
CHUNKS = 2
GROUP = 4

NEG_FILL = -1e30
BOTH = ("ctx", "exp")


def hop(block):
    devices = range(lax.axis_size("ctx"))
    return lax.ppermute(block, "ctx", [(i, i + 2) for i in devices if i + 2 in devices])


def swap(block):
    devices = range(lax.axis_size("ctx"))
    return lax.ppermute(block, "ctx", [(i, i ^ 1) for i in devices])


def attend_kernel(count, mask_ref, q_ref, *refs):
    k_refs, v_refs, out_ref = refs[:count], refs[count : 2 * count], refs[2 * count]
    allowed = mask_ref[...] > 0.0
    for head in range(GROUP):
        cols = slice(head * HEAD_DIM, (head + 1) * HEAD_DIM)
        query = q_ref[:, cols]
        scores = jnp.concatenate(
            [
                lax.dot_general(
                    query, k[:, cols], (((1,), (1,)), ((), ())), preferred_element_type=jnp.float32
                )
                for k in k_refs
            ],
            axis=1,
        ) * HEAD_DIM ** (-0.5)
        scores = jnp.where(allowed, scores, NEG_FILL)
        top = jnp.max(scores, axis=1, keepdims=True)
        probs = jnp.where(allowed, jnp.exp(scores - top), 0.0)
        total = jnp.sum(probs, axis=1, keepdims=True)
        low = probs.astype(jnp.bfloat16)
        rows = k_refs[0].shape[0]
        acc = sum(
            jnp.dot(
                low[:, i * rows : (i + 1) * rows], v[:, cols], preferred_element_type=jnp.float32
            )
            for i, v in enumerate(v_refs)
        )
        out_ref[:, cols] = (acc / total).astype(jnp.bfloat16)


def attend(mask, query, key_blocks, value_blocks):
    rows, width = query.shape
    count = len(key_blocks)
    wide = GROUP * HEAD_DIM
    block = pl.BlockSpec((rows, wide), lambda i: (0, i))
    return pl.pallas_call(
        functools.partial(attend_kernel, count),
        grid=(width // wide,),
        in_specs=[pl.BlockSpec(mask.shape, lambda i: (0, 0))] + [block] * (1 + 2 * count),
        out_specs=block,
        out_shape=jax.ShapeDtypeStruct((rows, width), jnp.bfloat16),
        compiler_params=pltpu.CompilerParams(vmem_limit_bytes=32 * 1024 * 1024),
        cost_estimate=pl.CostEstimate(
            flops=4 * rows * rows * count * width,
            bytes_accessed=4 * rows * width * (count + 1),
            transcendentals=rows * rows * count * HEADS,
        ),
    )(mask, query, *key_blocks, *value_blocks)


def gather_blocks(block):
    steps = lax.axis_size("ctx") // 4
    first = lax.axis_index("ctx") % 2 == 0
    chain = [block]
    for _ in range(steps):
        chain.append(hop(chain[-1]))
    others = [swap(chain[k]) for k in range(1, steps)]
    return chain + others + [swap(jnp.where(first, chain[0], chain[-1]))]


def expert_half(tokens, gate_up, down_rows):
    half = down_rows.shape[0]
    inner = jnp.dot(tokens, gate_up, preferred_element_type=jnp.float32)
    act = (jax.nn.silu(inner[:, :half]) * inner[:, half:]).astype(jnp.bfloat16)
    return jnp.dot(act, down_rows, preferred_element_type=jnp.float32)


def earlier(rows):
    order = jnp.arange(rows)
    return (order[:, None] < order[None, :]).astype(jnp.bfloat16)


def halved_sum(part, order):
    sizes = {"ctx": lax.axis_size("ctx"), "exp": lax.axis_size("exp")}
    left = [
        (axis, bit) for axis in BOTH for bit in reversed(range(sizes[axis].bit_length() - 1))
    ]
    block = part.reshape((2,) * len(left) + part.shape[1:])
    for axis, bit in order:
        place = left.index((axis, bit))
        left.pop(place)
        mine = (lax.axis_index(axis) >> bit) & 1
        kept = lax.dynamic_index_in_dim(block, mine, place, keepdims=False)
        sent = lax.dynamic_index_in_dim(block, 1 - mine, place, keepdims=False)
        pairs = [(i, i ^ (1 << bit)) for i in range(sizes[axis])]
        got = lax.ppermute(sent, axis, pairs)
        block = (kept.astype(jnp.float32) + got.astype(jnp.float32)).astype(jnp.bfloat16)
    return block


def routed_by_gather(normed, ids, codes, w_in, w_down):
    rows = normed.shape[0]
    owners = lax.axis_size("ctx") * lax.axis_size("exp")
    owner = lax.axis_index("ctx") * lax.axis_size("exp") + lax.axis_index("exp")
    blank = jnp.zeros((rows, HEAD_DIM - 2 * TOPK), jnp.bfloat16)
    wide = jnp.concatenate(
        [normed, ids.astype(jnp.bfloat16), codes.astype(jnp.bfloat16), blank], axis=1
    )
    w_wide = jnp.concatenate([w_in, jnp.zeros((HEAD_DIM, w_in.shape[1]), w_in.dtype)], axis=0)
    part_rows = rows // CHUNKS
    deep = [("ctx", bit) for bit in range(1, lax.axis_size("ctx").bit_length() - 1)]
    flat = [("exp", bit) for bit in range(lax.axis_size("exp").bit_length() - 1)]
    core = [("ctx", 0)]
    orders = [core + flat + deep, core + deep + flat[::-1]]
    pieces = []
    for c in range(CHUNKS):
        span = slice(c * part_rows, (c + 1) * part_rows)
        tokens = lax.all_gather(wide[span], BOTH, axis=0, tiled=True)
        named = tokens[:, D : D + TOPK].astype(jnp.int32) == owner // 2
        code = tokens[:, D + TOPK : D + 2 * TOPK].astype(jnp.float32)
        share = jnp.sum(jnp.where(named, code, 0.0), axis=1, keepdims=True) / jnp.sum(
            code, axis=1, keepdims=True
        )
        part = expert_half(tokens, w_wide, w_down)
        part = jnp.where(share > 0.0, part * share, 0.0).astype(jnp.bfloat16)
        pieces.append(halved_sum(part.reshape(owners, part_rows, D), orders[c % 2]))
    return jnp.concatenate(pieces, axis=0).astype(jnp.float32)


def routed_by_exchange(normed, ids, codes, capacity, w_in, w_down):
    rows = normed.shape[0]
    owners = lax.axis_size("ctx") * lax.axis_size("exp")
    experts = owners // 2
    codes = codes.astype(jnp.float32)
    route = codes / jnp.sum(codes, axis=1, keepdims=True)
    named = ids[:, :, None] == jnp.arange(experts, dtype=jnp.int32)
    member = jnp.any(named, axis=1)
    weight = jnp.sum(jnp.where(named, route[:, :, None], 0.0), axis=1)
    rank = jnp.einsum(
        "st,se->te", earlier(rows), member.astype(jnp.bfloat16), preferred_element_type=jnp.float32
    ).astype(jnp.int32)
    slot = jnp.where(member, rank, -1).T[:, None, :]
    chosen = slot == jnp.arange(capacity, dtype=jnp.int32)[None, :, None]
    sent = jnp.einsum(
        "ect,td->ecd", chosen.astype(jnp.bfloat16), normed, preferred_element_type=jnp.float32
    ).astype(jnp.bfloat16)
    sent = jnp.broadcast_to(sent[:, None], (experts, 2, capacity, D)).reshape(owners, capacity, D)
    got = lax.all_to_all(sent, BOTH, split_axis=0, concat_axis=0, tiled=True)
    part = expert_half(got.reshape(owners * capacity, D), w_in, w_down).astype(jnp.bfloat16)
    back = lax.all_to_all(
        part.reshape(owners, capacity, D), BOTH, split_axis=0, concat_axis=0, tiled=True
    ).reshape(experts, 2, capacity, D)
    expert_out = back[:, 0].astype(jnp.float32) + back[:, 1].astype(jnp.float32)
    spread = jnp.where(chosen, weight.T[:, None, :], 0.0)
    return jnp.einsum("ect,ecd->td", spread, expert_out, precision=lax.Precision.HIGHEST)


def local(
    queries,
    keys,
    values,
    segment_ids,
    hidden_in,
    out_weight,
    norm_gain,
    expert_ids,
    gate_codes,
    w_in,
    w_down,
):
    rows = queries.shape[1]
    ctx_size = lax.axis_size("ctx")
    exp_size = lax.axis_size("exp")
    owners = ctx_size * exp_size
    capacity = rows * TOPK * 8 // (3 * owners)
    me = lax.axis_index("ctx")
    steps = ctx_size // 4
    other = me + 1 - 2 * (me % 2)
    whose = jnp.stack(
        [me - 2 * k for k in range(steps + 1)]
        + [other - 2 * k for k in range(1, steps)]
        + [jnp.where(me % 2 == 0, other - 2 * steps, other)]
    )
    key_pos = (whose[:, None] * rows + jnp.arange(rows, dtype=jnp.int32)).reshape(-1)
    key_seg = jnp.concatenate(gather_blocks(segment_ids), axis=1)[0]
    query_pos = me * rows + jnp.arange(rows, dtype=jnp.int32)
    mask = (
        (key_pos[None, :] <= query_pos[:, None])
        & (key_pos[None, :] >= 0)
        & (key_seg[None, :] == segment_ids[0][:, None])
    ).astype(jnp.float32)
    attended = attend(mask, queries[0], gather_blocks(keys[0]), gather_blocks(values[0]))
    projected = jnp.dot(attended, out_weight, preferred_element_type=jnp.float32)
    mixed_wide = (
        (hidden_in[0].astype(jnp.float32) + projected).astype(jnp.bfloat16).astype(jnp.float32)
    )
    normed = (
        mixed_wide
        * lax.rsqrt(jnp.mean(mixed_wide * mixed_wide, axis=-1, keepdims=True) + 1e-06)
        * norm_gain
    ).astype(jnp.bfloat16)
    if 2 * capacity >= rows:
        routed = routed_by_gather(normed, expert_ids[0], gate_codes[0], w_in[0], w_down[0])
    else:
        routed = routed_by_exchange(
            normed, expert_ids[0], gate_codes[0], capacity, w_in[0], w_down[0]
        )
    return (mixed_wide + routed).astype(jnp.bfloat16)[None]


def solution(mesh):
    placed = (
        P("exp", "ctx", None),
        P("exp", "ctx", None),
        P("exp", "ctx", None),
        P("exp", "ctx"),
        P("exp", "ctx", None),
        P(),
        P(),
        P("exp", "ctx", None),
        P("exp", "ctx", None),
        P(("ctx", "exp"), None, None),
        P(("ctx", "exp"), None, None),
    )
    return jax.shard_map(
        local, mesh=mesh, in_specs=placed, out_specs=P("exp", "ctx", None), check_vma=False
    )
```

```python
import functools

import jax
import jax.numpy as jnp
from jax import lax
from jax.experimental import pallas as pl
from jax.experimental.pallas import tpu as pltpu
from jax.sharding import PartitionSpec as P

D = 2048
HEADS = 16
HEAD_DIM = 128
TOPK = 6
CHUNKS = 2
GROUP = 4

NEG_FILL = -1e30
BOTH = ("ctx", "exp")


def hop(block):
    devices = range(lax.axis_size("ctx"))
    return lax.ppermute(block, "ctx", [(i, i + 2) for i in devices if i + 2 in devices])


def swap(block):
    devices = range(lax.axis_size("ctx"))
    return lax.ppermute(block, "ctx", [(i, i ^ 1) for i in devices])


def attend_kernel(count, mask_ref, q_ref, *refs):
    k_refs, v_refs, out_ref = refs[:count], refs[count : 2 * count], refs[2 * count]
    allowed = mask_ref[...] > 0.0
    for head in range(GROUP):
        cols = slice(head * HEAD_DIM, (head + 1) * HEAD_DIM)
        query = q_ref[:, cols]
        scores = jnp.concatenate(
            [
                lax.dot_general(
                    query, k[:, cols], (((1,), (1,)), ((), ())), preferred_element_type=jnp.float32
                )
                for k in k_refs
            ],
            axis=1,
        ) * HEAD_DIM ** (-0.5)
        scores = jnp.where(allowed, scores, NEG_FILL)
        top = jnp.max(scores, axis=1, keepdims=True)
        probs = jnp.where(allowed, jnp.exp(scores - top), 0.0)
        total = jnp.sum(probs, axis=1, keepdims=True)
        low = probs.astype(jnp.bfloat16)
        rows = k_refs[0].shape[0]
        acc = sum(
            jnp.dot(
                low[:, i * rows : (i + 1) * rows], v[:, cols], preferred_element_type=jnp.float32
            )
            for i, v in enumerate(v_refs)
        )
        out_ref[:, cols] = (acc / total).astype(jnp.bfloat16)


def attend(mask, query, key_blocks, value_blocks):
    rows, width = query.shape
    count = len(key_blocks)
    wide = GROUP * HEAD_DIM
    block = pl.BlockSpec((rows, wide), lambda i: (0, i))
    return pl.pallas_call(
        functools.partial(attend_kernel, count),
        grid=(width // wide,),
        in_specs=[pl.BlockSpec(mask.shape, lambda i: (0, 0))] + [block] * (1 + 2 * count),
        out_specs=block,
        out_shape=jax.ShapeDtypeStruct((rows, width), jnp.bfloat16),
        compiler_params=pltpu.CompilerParams(vmem_limit_bytes=32 * 1024 * 1024),
        cost_estimate=pl.CostEstimate(
            flops=4 * rows * rows * count * width,
            bytes_accessed=4 * rows * width * (count + 1),
            transcendentals=rows * rows * count * HEADS,
        ),
    )(mask, query, *key_blocks, *value_blocks)


def gather_blocks(block):
    steps = lax.axis_size("ctx") // 4
    first = lax.axis_index("ctx") % 2 == 0
    chain = [block]
    for _ in range(steps):
        chain.append(hop(chain[-1]))
    others = [swap(chain[k]) for k in range(1, steps)]
    return chain + others + [swap(jnp.where(first, chain[0], chain[-1]))]


def expert_half(tokens, gate_up, down_rows):
    half = down_rows.shape[0]
    inner = jnp.dot(tokens, gate_up, preferred_element_type=jnp.float32)
    act = (jax.nn.silu(inner[:, :half]) * inner[:, half:]).astype(jnp.bfloat16)
    return jnp.dot(act, down_rows, preferred_element_type=jnp.float32)


def earlier(rows):
    order = jnp.arange(rows)
    return (order[:, None] < order[None, :]).astype(jnp.bfloat16)


def halved_sum(part, order):
    sizes = {"ctx": lax.axis_size("ctx"), "exp": lax.axis_size("exp")}
    left = [
        (axis, bit) for axis in BOTH for bit in reversed(range(sizes[axis].bit_length() - 1))
    ]
    left.remove(("ctx", 0))
    block = part.reshape((2,) * len(left) + part.shape[1:])
    for axis, bit in order:
        place = left.index((axis, bit))
        left.pop(place)
        mine = (lax.axis_index(axis) >> bit) & 1
        kept = lax.dynamic_index_in_dim(block, mine, place, keepdims=False)
        sent = lax.dynamic_index_in_dim(block, 1 - mine, place, keepdims=False)
        pairs = [(i, i ^ (1 << bit)) for i in range(sizes[axis])]
        got = lax.ppermute(sent, axis, pairs)
        block = (kept.astype(jnp.float32) + got.astype(jnp.float32)).astype(jnp.bfloat16)
    return block


def routed_by_gather(normed, ids, codes, w_in, w_down):
    rows = normed.shape[0]
    owners = lax.axis_size("ctx") * lax.axis_size("exp")
    owner = lax.axis_index("ctx") * lax.axis_size("exp") + lax.axis_index("exp")
    blank = jnp.zeros((rows, HEAD_DIM - 2 * TOPK), jnp.bfloat16)
    wide = jnp.concatenate(
        [normed, ids.astype(jnp.bfloat16), codes.astype(jnp.bfloat16), blank], axis=1
    )
    w_wide = jnp.concatenate([w_in, jnp.zeros((HEAD_DIM, w_in.shape[1]), w_in.dtype)], axis=0)
    part_rows = rows // CHUNKS
    deep = [("ctx", bit) for bit in range(1, lax.axis_size("ctx").bit_length() - 1)]
    flat = [("exp", bit) for bit in range(lax.axis_size("exp").bit_length() - 1)]
    orders = [flat + deep, deep + flat[::-1]]
    exp_size = lax.axis_size("exp")
    groups = [
        [i * exp_size + j for i in range(core, lax.axis_size("ctx"), 2) for j in range(exp_size)]
        for core in range(2)
    ]

    def shares(tokens):
        named = tokens[:, D : D + TOPK].astype(jnp.int32) == owner // 2
        code = tokens[:, D + TOPK : D + 2 * TOPK].astype(jnp.float32)
        share = jnp.sum(jnp.where(named, code, 0.0), axis=1, keepdims=True) / jnp.sum(
            code, axis=1, keepdims=True
        )
        part = expert_half(tokens, w_wide, w_down)
        return jnp.where(share > 0.0, part * share, 0.0).astype(jnp.bfloat16)

    pieces = []
    for c in range(CHUNKS):
        span = slice(c * part_rows, (c + 1) * part_rows)
        tokens = lax.all_gather(
            wide[span], BOTH, axis=0, tiled=True, axis_index_groups=groups
        )
        others = swap(tokens)
        mine = shares(tokens).astype(jnp.float32)
        got = swap(shares(others)).astype(jnp.float32)
        both = (mine + got).astype(jnp.bfloat16)
        pieces.append(halved_sum(both.reshape(owners // 2, part_rows, D), orders[c % 2]))
    return jnp.concatenate(pieces, axis=0).astype(jnp.float32)


def routed_by_exchange(normed, ids, codes, capacity, w_in, w_down):
    rows = normed.shape[0]
    owners = lax.axis_size("ctx") * lax.axis_size("exp")
    experts = owners // 2
    codes = codes.astype(jnp.float32)
    route = codes / jnp.sum(codes, axis=1, keepdims=True)
    named = ids[:, :, None] == jnp.arange(experts, dtype=jnp.int32)
    member = jnp.any(named, axis=1)
    weight = jnp.sum(jnp.where(named, route[:, :, None], 0.0), axis=1)
    rank = jnp.einsum(
        "st,se->te", earlier(rows), member.astype(jnp.bfloat16), preferred_element_type=jnp.float32
    ).astype(jnp.int32)
    slot = jnp.where(member, rank, -1).T[:, None, :]
    chosen = slot == jnp.arange(capacity, dtype=jnp.int32)[None, :, None]
    sent = jnp.einsum(
        "ect,td->ecd", chosen.astype(jnp.bfloat16), normed, preferred_element_type=jnp.float32
    ).astype(jnp.bfloat16)
    sent = jnp.broadcast_to(sent[:, None], (experts, 2, capacity, D)).reshape(owners, capacity, D)
    got = lax.all_to_all(sent, BOTH, split_axis=0, concat_axis=0, tiled=True)
    part = expert_half(got.reshape(owners * capacity, D), w_in, w_down).astype(jnp.bfloat16)
    back = lax.all_to_all(
        part.reshape(owners, capacity, D), BOTH, split_axis=0, concat_axis=0, tiled=True
    ).reshape(experts, 2, capacity, D)
    expert_out = back[:, 0].astype(jnp.float32) + back[:, 1].astype(jnp.float32)
    spread = jnp.where(chosen, weight.T[:, None, :], 0.0)
    return jnp.einsum("ect,ecd->td", spread, expert_out, precision=lax.Precision.HIGHEST)


def local(
    queries,
    keys,
    values,
    segment_ids,
    hidden_in,
    out_weight,
    norm_gain,
    expert_ids,
    gate_codes,
    w_in,
    w_down,
):
    rows = queries.shape[1]
    ctx_size = lax.axis_size("ctx")
    exp_size = lax.axis_size("exp")
    owners = ctx_size * exp_size
    capacity = rows * TOPK * 8 // (3 * owners)
    me = lax.axis_index("ctx")
    steps = ctx_size // 4
    other = me + 1 - 2 * (me % 2)
    whose = jnp.stack(
        [me - 2 * k for k in range(steps + 1)]
        + [other - 2 * k for k in range(1, steps)]
        + [jnp.where(me % 2 == 0, other - 2 * steps, other)]
    )
    key_pos = (whose[:, None] * rows + jnp.arange(rows, dtype=jnp.int32)).reshape(-1)
    key_seg = jnp.concatenate(gather_blocks(segment_ids), axis=1)[0]
    query_pos = me * rows + jnp.arange(rows, dtype=jnp.int32)
    mask = (
        (key_pos[None, :] <= query_pos[:, None])
        & (key_pos[None, :] >= 0)
        & (key_seg[None, :] == segment_ids[0][:, None])
    ).astype(jnp.float32)
    attended = attend(mask, queries[0], gather_blocks(keys[0]), gather_blocks(values[0]))
    projected = jnp.dot(attended, out_weight, preferred_element_type=jnp.float32)
    mixed_wide = (
        (hidden_in[0].astype(jnp.float32) + projected).astype(jnp.bfloat16).astype(jnp.float32)
    )
    normed = (
        mixed_wide
        * lax.rsqrt(jnp.mean(mixed_wide * mixed_wide, axis=-1, keepdims=True) + 1e-06)
        * norm_gain
    ).astype(jnp.bfloat16)
    if 2 * capacity >= rows:
        routed = routed_by_gather(normed, expert_ids[0], gate_codes[0], w_in[0], w_down[0])
    else:
        routed = routed_by_exchange(
            normed, expert_ids[0], gate_codes[0], capacity, w_in[0], w_down[0]
        )
    return (mixed_wide + routed).astype(jnp.bfloat16)[None]


def solution(mesh):
    placed = (
        P("exp", "ctx", None),
        P("exp", "ctx", None),
        P("exp", "ctx", None),
        P("exp", "ctx"),
        P("exp", "ctx", None),
        P(),
        P(),
        P("exp", "ctx", None),
        P("exp", "ctx", None),
        P(("ctx", "exp"), None, None),
        P(("ctx", "exp"), None, None),
    )
    return jax.shard_map(
        local, mesh=mesh, in_specs=placed, out_specs=P("exp", "ctx", None), check_vma=False
    )
```
